32 devices in a mesh: row: 8 (over z, y), col: 4 (over x, core).
Axes of the slice: x: 2, y: 2, z: 4, core: 2. Of those that a mesh axis runs over, the one named last changes fastest.
Arguments:
- upper_tiles: bfloat16 [256, 17, 4096], P(('row', 'col')), may hold values from -0.51 to 0.51, as said below
- block_columns: int32 [256, 17], P(('row', 'col')), may hold values from -1 to 255, as said below
Outputs:
- new_tiles: float32 [256, 17, 4096], P(('row', 'col'))
- occupancy: float32 [], replicated
The draws below stay inside these ranges and needn't reach their ends.
Inputs may be any that keep to these rules, and one draw needn't show every extreme that they name: `block_columns`: slot 0 of block row i holds i. The following slots hold distinct block columns (i + s) mod 256 with 1 <= s <= 16, in increasing s, and the remaining slots hold -1. Some block rows fill all 17 slots. `upper_tiles`: the block in slot 0 is symmetric.
All inputs are finite; a program needn't handle non-finite values.
Results may differ from the reference program's by a relative error of at most 0.0003.
Values may be sent and summed in bfloat16 or wider, within the bound.
A program may use at most 128 MiB of HBM per device.

```python
import jax
import jax.numpy as jnp
import numpy as np
from jax import lax

BLOCK = 64
HALF = 16
ROWS_DEV = 8
NBLOCKS = 256
SLOTS = 17
ORDER = 16384


def draw_block_columns(key, part):
    row_ids = jnp.arange(NBLOCKS, dtype=jnp.int32)
    threshold = 20 + 75 * row_ids // NBLOCKS
    chances = jax.random.randint(key, (NBLOCKS, HALF), 0, 100, dtype=jnp.int32)
    kept_mask = (chances < threshold[:, None]) | (row_ids % 7 == 0)[:, None]
    offsets = jnp.arange(1, HALF + 1, dtype=jnp.int32)[None, :]
    ranked = jnp.sort(jnp.where(kept_mask, offsets, offsets + HALF + 1), axis=1)
    listed = jnp.where(ranked <= HALF, (row_ids[:, None] + ranked) % NBLOCKS, -1)
    return jnp.concatenate([row_ids[:, None], listed], axis=1).astype(jnp.int32)


def draw_upper_tiles(key, part):
    tile_values = jax.random.truncated_normal(key, -6.0, 6.0, (NBLOCKS, SLOTS, BLOCK * BLOCK), jnp.float32) * 0.06
    diagonal = tile_values[:, 0].reshape(NBLOCKS, BLOCK, BLOCK)
    diagonal = (diagonal + jnp.swapaxes(diagonal, 1, 2)) * 0.7071
    tile_values = jnp.concatenate([diagonal.reshape(NBLOCKS, 1, BLOCK * BLOCK), tile_values[:, 1:]], axis=1)
    return tile_values.astype(jnp.bfloat16)


def setup_inputs(seed: int = 0) -> dict:
    arg_keys = jax.random.split(jax.random.key(seed), 3)
    upper_tiles = draw_upper_tiles(jax.random.fold_in(arg_keys[2], 71), 0)
    block_columns = draw_block_columns(jax.random.fold_in(arg_keys[2], 71), 0)
    return dict(upper_tiles=upper_tiles, block_columns=block_columns)


def entry_tables(rows_dev, half):
    band_width = half + 1
    window = rows_dev + 2 * half
    zero_index = window * band_width

    def lookup(row_pos, col_pos):
        if col_pos >= row_pos and col_pos - row_pos <= half:
            return row_pos * band_width + col_pos - row_pos, False
        if col_pos < row_pos and row_pos - col_pos <= half:
            return col_pos * band_width + row_pos - col_pos, True
        return zero_index, False

    left_index = np.zeros((rows_dev, window), np.int32)
    left_flip = np.zeros((rows_dev, window), np.bool_)
    for own_row in range(rows_dev):
        for other_row in range(window):
            left_index[own_row, other_row], left_flip[own_row, other_row] = lookup(half + own_row, other_row)
    right_index = np.zeros((window, rows_dev + half), np.int32)
    right_flip = np.zeros((window, rows_dev + half), np.bool_)
    for other_row in range(window):
        for column_pos in range(rows_dev + half):
            right_index[other_row, column_pos], right_flip[other_row, column_pos] = lookup(other_row, half + column_pos)
    return left_index, left_flip, right_index, right_flip


def flip_tiles(tiles, block):
    shaped = tiles.reshape(tiles.shape[:-1] + (block, block))
    return jnp.swapaxes(shaped, -1, -2).reshape(tiles.shape)


def reference(upper_tiles, block_columns):
    tile_size = BLOCK * BLOCK
    window_rows = ROWS_DEV + 2 * HALF
    span_cols = ROWS_DEV + HALF
    row_ids = jnp.arange(NBLOCKS, dtype=jnp.int32)
    slot_range = jnp.arange(SLOTS, dtype=jnp.int32)
    listed = block_columns >= 0
    offsets_of = jnp.mod(block_columns - row_ids[:, None], NBLOCKS).astype(jnp.int32)
    matches = listed[:, :, None] & (offsets_of[:, :, None] == slot_range[None, None, :])
    slot_of = jnp.sum(jnp.where(matches, slot_range[None, :, None], 0), axis=1).astype(jnp.int32)
    present = jnp.any(matches, axis=1)
    band = jax.vmap(lambda tiles, picks: tiles[picks])(upper_tiles, slot_of)
    band = jnp.where(present[:, :, None], band, jnp.zeros((), upper_tiles.dtype))
    padded = jnp.concatenate([band[NBLOCKS - HALF:], band, band[:HALF]], axis=0)
    left_np, left_flip_np, right_np, right_flip_np = entry_tables(ROWS_DEV, HALF)
    left_index = jnp.asarray(left_np)
    left_flip = jnp.asarray(left_flip_np)
    right_index = jnp.asarray(right_np)
    right_flip = jnp.asarray(right_flip_np)
    local_rows = jnp.arange(ROWS_DEV, dtype=jnp.int32)

    def one_group(group):
        start = (group * ROWS_DEV).astype(jnp.int32)
        window = lax.dynamic_slice_in_dim(padded, start, window_rows, 0)
        flat = jnp.concatenate([window.reshape(window_rows * SLOTS, tile_size), jnp.zeros((1, tile_size), window.dtype)], axis=0)
        left = flat[left_index]
        left = jnp.where(left_flip[:, :, None], flip_tiles(left, BLOCK), left)
        right = flat[right_index]
        right = jnp.where(right_flip[:, :, None], flip_tiles(right, BLOCK), right)
        left = left.astype(jnp.float32).reshape(ROWS_DEV, window_rows, BLOCK, BLOCK)
        right = right.astype(jnp.float32).reshape(window_rows, span_cols, BLOCK, BLOCK)
        product = jnp.einsum("rjab,jkbc->rkac", left, right, precision=lax.Precision.HIGHEST)
        product = product.reshape(ROWS_DEV, span_cols, tile_size)
        own_tiles = lax.dynamic_slice_in_dim(upper_tiles, start, ROWS_DEV, 0)
        own_columns = lax.dynamic_slice_in_dim(block_columns, start, ROWS_DEV, 0)
        own_ids = start + local_rows
        own_valid = own_columns >= 0
        own_offsets = jnp.mod(own_columns - own_ids[:, None], NBLOCKS).astype(jnp.int32)
        target = jnp.where(own_valid, own_offsets + local_rows[:, None], 0).astype(jnp.int32)
        picked = jax.vmap(lambda rows_of, picks: rows_of[picks])(product, target)
        fresh = jnp.where(own_valid[:, :, None], 2.0 * own_tiles.astype(jnp.float32) - picked, jnp.zeros((), jnp.float32))
        diag_product = product[local_rows, local_rows].reshape(ROWS_DEV, BLOCK, BLOCK)
        diag_own = own_tiles[:, 0].astype(jnp.float32).reshape(ROWS_DEV, BLOCK, BLOCK)
        trace_part = jnp.sum(2.0 * jnp.diagonal(diag_own, axis1=1, axis2=2) - jnp.diagonal(diag_product, axis1=1, axis2=2))
        return fresh, trace_part

    fresh_all, traces = lax.map(one_group, jnp.arange(NBLOCKS // ROWS_DEV, dtype=jnp.int32))
    new_tiles = fresh_all.reshape(NBLOCKS, SLOTS, tile_size)
    occupancy = (jnp.sum(traces) / ORDER).astype(jnp.float32)
    return new_tiles, occupancy
```

```python
import functools
import math

import jax
import jax.numpy as jnp
from jax import lax
from jax.experimental import pallas as pl
from jax.experimental.pallas import tpu as pltpu
from jax.sharding import PartitionSpec as P

MESH = pl.DeviceIdType.MESH
F32 = jnp.float32
BF16 = jnp.bfloat16


def dot(a, b, ca, cb):
    return lax.dot_general(a, b, (((ca,), (cb,)), ((), ())), preferred_element_type=F32)


def kernel(
    dims,
    x_ref,
    cols_ref,
    out_ref,
    tab,
    stage,
    flat,
    own,
    sym,
    e1,
    f1,
    e2,
    d1,
    c1,
    d2,
    prod,
    send_sem,
    recv_sem,
):
    rows, slots, block, nrow, ncol = dims
    half = slots - 1
    width = rows * block
    span = rows + half
    devices = nrow * ncol
    nblocks = devices * rows
    lanes = 2 * block
    me = lax.axis_index("row") * ncol + lax.axis_index("col")

    def at(shift):
        other = lax.rem(me + shift + devices, devices)
        return (lax.div(other, ncol), lax.rem(other, ncol))

    barrier = pltpu.get_barrier_semaphore()
    for shift in (-2, -1, 1, 2):
        pl.semaphore_signal(barrier, inc=1, device_id=at(shift), device_id_type=MESH)

    def fill(r, carry):
        row_id = me * rows + r
        for t in range(rows + span):
            tab[r, t] = jnp.int32(-1)
        tab[r, rows] = jnp.where(cols_ref[r, 0] >= 0, 0, -1).astype(jnp.int32)
        slot = jnp.int32(1)
        for offset in range(1, half + 1):
            want = row_id + offset
            want = jnp.where(want >= nblocks, want - nblocks, want)
            hit = cols_ref[r, jnp.minimum(slot, half)] == want
            tab[r, rows + offset] = jnp.where(hit, slot, -1)
            slot = slot + hit.astype(jnp.int32)
        return carry

    lax.fori_loop(0, rows, fill, 0)

    left = lax.broadcasted_iota(jnp.int32, (block // 2, lanes), 1) < block

    def unpack(r, carry):
        for m in range(span // 2):
            pair = []
            for k in (2 * m, 2 * m + 1):
                slot = tab[r, rows + k - r]
                tile = x_ref[jnp.clip(slot, 0, half), r].astype(F32)
                pair.append(jnp.where(slot >= 0, tile, 0.0))
            even = jnp.where(left, pair[0], pltpu.roll(pair[1], block, 1))
            odd = jnp.where(left, pltpu.roll(pair[0], block, 1), pair[1])
            stage[m, pl.ds(0, block // 2, stride=2), :] = even
            stage[m, pl.ds(1, block // 2, stride=2), :] = odd
        for m in range(span // 2):
            own[pl.ds(pl.multiple_of(r * block, block), block), m * lanes : (m + 1) * lanes] = stage[m].astype(BF16)
        return carry

    lax.fori_loop(0, rows, unpack, 0)

    for q in range(rows // 2):
        strip = pl.ds(q * lanes, lanes)
        if q:
            d1[strip, : q * lanes] = jnp.zeros((lanes, q * lanes), BF16)
            d2[strip, : q * lanes] = jnp.zeros((lanes, q * lanes), BF16)
        if (q + 1) * lanes < width:
            f1[strip, (q + 1) * lanes :] = jnp.zeros((lanes, width - (q + 1) * lanes), BF16)
            e2[strip, (q + 1) * lanes :] = jnp.zeros((lanes, width - (q + 1) * lanes), BF16)

    pl.semaphore_wait(barrier, 4)

    copies = {}
    plan = (
        ("e1", e1, 1, 1, "full"),
        ("c1", c1, 1, -1, "full"),
        ("f1", f1, 2, 1, "low"),
        ("d1", d1, 0, -1, "up"),
        ("e2", e2, 2, 2, "low"),
        ("d2", d2, 0, -2, "up"),
    )
    for index, (name, target, part, shift, kind) in enumerate(plan):
        copies[name] = []
        for q in range(rows // 2):
            lo = q * lanes if kind == "up" else 0
            size = {"full": width, "up": width - q * lanes, "low": (q + 1) * lanes}[kind]
            copy = pltpu.make_async_remote_copy(
                src_ref=own.at[pl.ds(q * lanes, lanes), pl.ds(part * width + lo, size)],
                dst_ref=target.at[pl.ds(q * lanes, lanes), pl.ds(lo, size)],
                send_sem=send_sem.at[index, q],
                recv_sem=recv_sem.at[index, q],
                device_id=at(shift),
                device_id_type=MESH,
            )
            copy.start()
            copies[name].append(copy)

    def arrived(*names):
        for name in names:
            for copy in copies[name]:
                copy.wait_recv()

    row_block = lax.broadcasted_iota(jnp.int32, (width, width), 0) // block
    col_block = lax.broadcasted_iota(jnp.int32, (width, width), 1) // block
    upper = row_block <= col_block

    def symmetric(d):
        d = d.astype(F32)
        return jnp.where(upper, d, d.T).astype(BF16)

    sym[...] = symmetric(own[:, :width])
    a = own.at[:, width : 2 * width]
    b = own.at[:, 2 * width :]
    p0, p1, p2 = (prod.at[:, i * width : (i + 1) * width] for i in range(3))
    p0[...] = dot(sym[...], sym[...], 1, 0) + dot(a[...], a[...], 1, 1) + dot(b[...], b[...], 1, 1)
    p1[...] = dot(sym[...], a[...], 1, 0)
    p2[...] = dot(sym[...], b[...], 1, 0)

    arrived("e1")
    p0[...] += dot(e1[...], e1[...], 0, 0)
    arrived("c1")
    p1[...] += dot(b[...], c1[...], 1, 1)
    p2[...] += dot(a[...], c1[...], 1, 0)
    arrived("f1")
    p1[...] += dot(e1[...], f1[...], 0, 0)
    arrived("d1")
    sym[...] = symmetric(d1[...])
    p1[...] += dot(a[...], sym[...], 1, 0)
    arrived("e2")
    p0[...] += dot(e2[...], e2[...], 0, 0)
    arrived("d2")
    sym[...] = symmetric(d2[...])
    p2[...] += dot(b[...], sym[...], 1, 0)

    def pack(r, carry):
        rs = pl.ds(pl.multiple_of(r * block, block), block)
        for m in range(span // 2):
            cs = slice(m * lanes, (m + 1) * lanes)
            stage[m] = 2.0 * own[rs, cs].astype(F32) - prod[rs, cs]
        for m in range(span // 2):
            even = stage[m, pl.ds(0, block // 2, stride=2), :]
            odd = stage[m, pl.ds(1, block // 2, stride=2), :]
            flat[2 * m] = jnp.where(left, even, pltpu.roll(odd, block, 1))
            flat[2 * m + 1] = jnp.where(left, pltpu.roll(even, block, 1), odd)
        row_id = me * rows + r
        for s in range(slots):
            column = cols_ref[r, s]
            offset = column - row_id
            offset = jnp.where(offset < 0, offset + nblocks, offset)
            offset = jnp.where(column >= 0, jnp.minimum(offset, half), 0)
            out_ref[s, r] = jnp.where(column >= 0, flat[r + offset], 0.0)
        return carry

    lax.fori_loop(0, rows, pack, 0)

    for group in copies.values():
        for copy in group:
            copy.wait_send()


def body(nrow, ncol, upper_tiles, block_columns):
    rows, slots, tile_size = upper_tiles.shape
    block = math.isqrt(tile_size)
    half = slots - 1
    assert half == 2 * rows and rows % 2 == 0 and 2 * block == 128
    lanes = 2 * block
    width = rows * block
    span = rows + half

    listed = block_columns >= 0
    tiles = upper_tiles.astype(F32)
    weight = jnp.where(listed, jnp.where(jnp.arange(slots) == 0, 1.0, 2.0), 0.0)
    squares = jnp.sum(tiles * tiles * weight[:, :, None])
    on_diagonal = (jnp.arange(tile_size) % (block + 1) == 0) & True
    doubled = 2.0 * jnp.sum(jnp.where(on_diagonal, tiles[:, 0], 0.0))
    total = lax.psum(doubled - squares, ("row", "col"))
    occupancy = (total / (nrow * ncol * rows * block)).astype(F32)

    square = pltpu.VMEM((width, width), BF16)
    new = pl.pallas_call(
        functools.partial(kernel, (rows, slots, block, nrow, ncol)),
        out_shape=jax.ShapeDtypeStruct((slots, rows, block // 2, lanes), F32),
        in_specs=[pl.BlockSpec(memory_space=pltpu.VMEM), pl.BlockSpec(memory_space=pltpu.SMEM)],
        out_specs=pl.BlockSpec(memory_space=pltpu.VMEM),
        scratch_shapes=[
            pltpu.SMEM((rows, rows + span), jnp.int32),
            pltpu.VMEM((span // 2, block, lanes), F32),
            pltpu.VMEM((span, block // 2, lanes), F32),
            pltpu.VMEM((width, 3 * width), BF16),
            square,
            square,
            square,
            square,
            square,
            square,
            square,
            pltpu.VMEM((width, 3 * width), F32),
            pltpu.SemaphoreType.DMA((6, rows // 2)),
            pltpu.SemaphoreType.DMA((6, rows // 2)),
        ],
        compiler_params=pltpu.CompilerParams(
            collective_id=0, has_side_effects=True, vmem_limit_bytes=48 * 1024 * 1024
        ),
        cost_estimate=pl.CostEstimate(
            flops=24 * width**3, bytes_accessed=6 * rows * slots * tile_size, transcendentals=0
        ),
    )(upper_tiles.swapaxes(0, 1).reshape(slots, rows, block // 2, lanes), block_columns)
    return new.reshape(slots, rows, tile_size).swapaxes(0, 1), occupancy


def solution(mesh):
    placed = (P(("row", "col"), None, None), P(("row", "col"), None))
    return jax.shard_map(
        functools.partial(body, mesh.shape["row"], mesh.shape["col"]),
        mesh=mesh,
        in_specs=placed,
        out_specs=(P(("row", "col"), None, None), P()),
        check_vma=False,
    )
```

```python
import functools
import math

import jax
import jax.numpy as jnp
from jax import lax
from jax.experimental import pallas as pl
from jax.experimental.pallas import tpu as pltpu
from jax.sharding import PartitionSpec as P

MESH = pl.DeviceIdType.MESH
F32 = jnp.float32
BF16 = jnp.bfloat16


def dot(a, b, ca, cb):
    return lax.dot_general(a, b, (((ca,), (cb,)), ((), ())), preferred_element_type=F32)


def kernel(
    dims,
    x_ref,
    cols_ref,
    out_ref,
    occupancy_ref,
    tab,
    stage,
    flat,
    own,
    e1,
    f1,
    e2,
    d1,
    c1,
    d2,
    prod,
    col_parts,
    row_parts,
    send_sem,
    recv_sem,
    col_send,
    col_recv,
    row_send,
    row_recv,
):
    rows, slots, block, nrow, ncol = dims
    half = slots - 1
    width = rows * block
    span = rows + half
    devices = nrow * ncol
    nblocks = devices * rows
    lanes = 2 * block
    strips = rows // 2
    my_row = lax.axis_index("row")
    my_col = lax.axis_index("col")
    me = my_row * ncol + my_col
    even_device = lax.rem(my_col, 2) == 0

    def at(shift):
        other = lax.rem(me + shift + devices, devices)
        return (lax.div(other, ncol), lax.rem(other, ncol))

    def col_peer(d):
        return lax.rem(my_col + d, ncol)

    def row_peer(d):
        return lax.rem(my_row + d, nrow)

    barrier = pltpu.get_barrier_semaphore()
    peers = [at(shift) for shift in (-2, -1, 1, 2)]
    peers += [(my_row, col_peer(d)) for d in range(1, ncol)]
    peers += [(row_peer(d), my_col) for d in range(1, nrow)]
    for peer in peers:
        pl.semaphore_signal(barrier, inc=1, device_id=peer, device_id_type=MESH)

    def fill(r, carry):
        row_id = me * rows + r
        tab[r, 0] = jnp.where(cols_ref[r, 0] >= 0, 0, -1).astype(jnp.int32)
        slot = jnp.int32(1)
        for offset in range(1, half + 1):
            want = row_id + offset
            want = jnp.where(want >= nblocks, want - nblocks, want)
            hit = cols_ref[r, jnp.minimum(slot, half)] == want
            tab[r, offset] = jnp.where(hit, slot, -1)
            slot = slot + hit.astype(jnp.int32)
        return carry

    lax.fori_loop(0, rows, fill, 0)

    sub = lax.broadcasted_iota(jnp.int32, (block // 2, lanes), 0)
    lane = lax.broadcasted_iota(jnp.int32, (block // 2, lanes), 1)
    left = lane < block
    on_diagonal = lane == 2 * sub + jnp.where(left, 0, block + 1)

    targets = {"f1": (f1, 2, 1, "low"), "d1": (d1, 0, -1, "up"), "e2": (e2, 2, 2, "low"),
               "d2": (d2, 0, -2, "up"), "e1": (e1, 1, 1, "full"), "c1": (c1, 1, -1, "full")}
    order = tuple(targets)

    def ranges(kind, q):
        lo = q * lanes if kind == "up" else 0
        return lo, {"full": width, "up": width - q * lanes, "low": (q + 1) * lanes}[kind]

    def strip_copy(name, q):
        target, part, shift, kind = targets[name]
        lo, size = ranges(kind, q)
        return pltpu.make_async_remote_copy(
            src_ref=own.at[pl.ds(q * lanes, lanes), pl.ds(part * width + lo, size)],
            dst_ref=target.at[pl.ds(q * lanes, lanes), pl.ds(lo, size)],
            send_sem=send_sem.at[order.index(name), q],
            recv_sem=recv_sem.at[order.index(name), q],
            device_id=at(shift),
            device_id_type=MESH,
        )

    def forward_copy(name, q):
        source, goal, shift = (f1, "e2", 1) if name == "f1" else (d1, "d2", -1)
        lo, size = ranges(targets[name][3], q)
        where = (pl.ds(q * lanes, lanes), pl.ds(lo, size))
        return pltpu.make_async_remote_copy(
            src_ref=source.at[where],
            dst_ref=targets[goal][0].at[where],
            send_sem=send_sem.at[len(order), q],
            recv_sem=recv_sem.at[order.index(goal), q],
            device_id=at(shift),
            device_id_type=MESH,
        )

    total = jnp.zeros((block // 2, lanes), F32)
    for q in range(strips):
        for r in (2 * q, 2 * q + 1):
            for m in range(span // 2):
                cs = slice(m * lanes, (m + 1) * lanes)
                pair = []
                for k in (2 * m, 2 * m + 1):
                    offset = k - r
                    if offset < 0 or offset > half:
                        pair.append(None)
                        continue
                    slot = tab[r, offset]
                    tile = x_ref[jnp.clip(slot, 0, half), r].astype(F32)
                    tile = jnp.where(slot >= 0, tile, 0.0)
                    if offset == 0:
                        total = total + jnp.where(on_diagonal, 2.0 * tile, 0.0) - tile * tile
                    else:
                        total = total - 2.0 * (tile * tile)
                    pair.append(tile)
                if pair[0] is None and pair[1] is None:
                    own[r * block : (r + 1) * block, cs] = jnp.zeros((block, lanes), BF16)
                    continue
                pair = [jnp.zeros((block // 2, lanes), F32) if t is None else t for t in pair]
                place = (r % 2) * (span // 2) + m
                stage[place, pl.ds(0, block // 2, stride=2), :] = jnp.where(left, pair[0], pltpu.roll(pair[1], block, 1))
                stage[place, pl.ds(1, block // 2, stride=2), :] = jnp.where(left, pltpu.roll(pair[0], block, 1), pair[1])
                own[r * block : (r + 1) * block, cs] = stage[place].astype(BF16)
        if q == 0:
            pl.semaphore_wait(barrier, len(peers))
        strip_copy("f1", q).start()
        strip_copy("d1", q).start()

        @pl.when(even_device)
        def _():
            strip_copy("e2", q).start()

        @pl.when(jnp.logical_not(even_device))
        def _():
            strip_copy("d2", q).start()

        strip_copy("e1", q).start()
        strip_copy("c1", q).start()

    part = total[0:8]
    for i in range(1, block // 16):
        part = part + total[8 * i : 8 * i + 8]

    def col_copy(d, mine):
        return pltpu.make_async_remote_copy(
            src_ref=col_parts.at[my_col],
            dst_ref=col_parts.at[my_col if mine else col_peer(ncol - d)],
            send_sem=col_send.at[d],
            recv_sem=col_recv.at[d],
            device_id=(my_row, col_peer(d)),
            device_id_type=MESH,
        )

    def row_copy(d, mine):
        return pltpu.make_async_remote_copy(
            src_ref=row_parts.at[my_row],
            dst_ref=row_parts.at[my_row if mine else row_peer(nrow - d)],
            send_sem=row_send.at[d],
            recv_sem=row_recv.at[d],
            device_id=(row_peer(d), my_col),
            device_id_type=MESH,
        )

    col_parts[my_col] = part
    for d in range(1, ncol):
        col_copy(d, True).start()

    def panel(i):
        return prod.at[:, i * width : (i + 1) * width]

    p0, p1, p2 = panel(0), panel(1), panel(2)
    d = own.at[:, :width]
    a = own.at[:, width : 2 * width]
    b = own.at[:, 2 * width :]

    corner = (
        lax.broadcasted_iota(jnp.int32, (lanes, lanes), 0) // block
        <= lax.broadcasted_iota(jnp.int32, (lanes, lanes), 1) // block
    )

    def symmetric_tile(upper):
        upper = upper.astype(F32)
        return jnp.where(corner, upper, upper.T).astype(BF16)

    def times_symmetric(x, u, p, q):
        lo, hi = q * lanes, (q + 1) * lanes
        rs = slice(lo, hi)
        tile = symmetric_tile(u[rs, lo:hi])
        p[:, rs] += dot(x[:, rs], tile, 1, 0)
        if hi < width:
            p[:, rs] += dot(x[:, hi:], u[rs, hi:], 1, 1)
            p[:, hi:] += dot(x[:, rs], u[rs, hi:], 1, 0)

    p0[...] = dot(a[...], a[...], 1, 1) + dot(b[...], b[...], 1, 1)
    full = d[...].astype(F32)
    block_upper = (
        lax.broadcasted_iota(jnp.int32, (width, width), 0) // block
        <= lax.broadcasted_iota(jnp.int32, (width, width), 1) // block
    )
    full = jnp.where(block_upper, full, full.T).astype(BF16)
    p0[...] += dot(full, full, 1, 0)
    p1[...] = dot(full, a[...], 1, 0)
    p2[...] = dot(full, b[...], 1, 0)

    for i in range(1, ncol):
        col_copy(i, False).wait_recv()
    part = col_parts[0]
    for i in range(1, ncol):
        part = part + col_parts[i]
    row_parts[my_row] = part
    for i in range(1, nrow):
        row_copy(i, True).start()

    for q in range(strips):
        rs = slice(q * lanes, (q + 1) * lanes)
        low = slice(0, (q + 1) * lanes)
        strip_copy("f1", q).wait_recv()

        @pl.when(even_device)
        def _():
            forward_copy("f1", q).start()

        strip_copy("d1", q).wait_recv()

        @pl.when(jnp.logical_not(even_device))
        def _():
            forward_copy("d1", q).start()

        times_symmetric(a, d1, p1, q)
        strip_copy("e1", q).wait_recv()
        p0[...] += dot(e1[rs, :], e1[rs, :], 0, 0)
        p1[:, low] += dot(e1[rs, :], f1[rs, low], 0, 0)
        strip_copy("c1", q).wait_recv()
        p1[:, rs] += dot(b[...], c1[rs, :], 1, 1)
        p2[...] += dot(a[:, rs], c1[rs, :], 1, 0)
    for q in range(strips):
        rs = slice(q * lanes, (q + 1) * lanes)
        low = slice(0, (q + 1) * lanes)
        strip_copy("e2", q).wait_recv()
        p0[low, low] += dot(e2[rs, low], e2[rs, low], 0, 0)
        strip_copy("d2", q).wait_recv()
        times_symmetric(b, d2, p2, q)

    for r in range(rows):
        for m in range(r // 2, (r + half) // 2 + 1):
            cs = slice(m * lanes, (m + 1) * lanes)
            place = (r % 2) * (span // 2) + m
            stage[place] = prod[r * block : (r + 1) * block, cs]
            even = stage[place, pl.ds(0, block // 2, stride=2), :]
            odd = stage[place, pl.ds(1, block // 2, stride=2), :]
            flat[r, 2 * m] = jnp.where(left, even, pltpu.roll(odd, block, 1))
            flat[r, 2 * m + 1] = jnp.where(left, pltpu.roll(even, block, 1), odd)

    def pick(r, carry):
        row_id = me * rows + r
        for s in range(slots):
            column = cols_ref[r, s]
            offset = column - row_id
            offset = jnp.where(offset < 0, offset + nblocks, offset)
            offset = jnp.where(column >= 0, jnp.minimum(offset, half), 0)
            fresh = 2.0 * x_ref[s, r].astype(F32) - flat[r, r + offset]
            out_ref[s, r] = jnp.where(column >= 0, fresh, 0.0)
        return carry

    lax.fori_loop(0, rows, pick, 0)

    for i in range(1, nrow):
        row_copy(i, False).wait_recv()
    part = row_parts[0]
    for i in range(1, nrow):
        part = part + row_parts[i]
    occupancy_ref[0, 0] = jnp.sum(part) * (1.0 / (nblocks * block))

    for q in range(strips):
        for name in ("f1", "d1", "e1", "c1"):
            strip_copy(name, q).wait_send()

        @pl.when(even_device)
        def _():
            strip_copy("e2", q).wait_send()
            forward_copy("f1", q).wait_send()

        @pl.when(jnp.logical_not(even_device))
        def _():
            strip_copy("d2", q).wait_send()
            forward_copy("d1", q).wait_send()

    for i in range(1, ncol):
        col_copy(i, True).wait_send()
    for i in range(1, nrow):
        row_copy(i, True).wait_send()


def body(nrow, ncol, upper_tiles, block_columns):
    rows, slots, tile_size = upper_tiles.shape
    block = math.isqrt(tile_size)
    half = slots - 1
    assert half == 2 * rows and rows % 2 == 0 and 2 * block == 128 and ncol % 2 == 0
    lanes = 2 * block
    width = rows * block
    span = rows + half
    strips = rows // 2

    square = pltpu.VMEM((width, width), BF16)
    new, occupancy = pl.pallas_call(
        functools.partial(kernel, (rows, slots, block, nrow, ncol)),
        out_shape=(
            jax.ShapeDtypeStruct((slots, rows, block // 2, lanes), F32),
            jax.ShapeDtypeStruct((1, 1), F32),
        ),
        in_specs=[pl.BlockSpec(memory_space=pltpu.VMEM), pl.BlockSpec(memory_space=pltpu.SMEM)],
        out_specs=(pl.BlockSpec(memory_space=pltpu.VMEM), pl.BlockSpec(memory_space=pltpu.SMEM)),
        scratch_shapes=[
            pltpu.SMEM((rows, slots), jnp.int32),
            pltpu.VMEM((span, block, lanes), F32),
            pltpu.VMEM((rows, span, block // 2, lanes), F32),
            pltpu.VMEM((width, 3 * width), BF16),
            square,
            square,
            square,
            square,
            square,
            square,
            pltpu.VMEM((width, 3 * width), F32),
            pltpu.VMEM((ncol, 8, lanes), F32),
            pltpu.VMEM((nrow, 8, lanes), F32),
            pltpu.SemaphoreType.DMA((7, strips)),
            pltpu.SemaphoreType.DMA((6, strips)),
            pltpu.SemaphoreType.DMA((ncol,)),
            pltpu.SemaphoreType.DMA((ncol,)),
            pltpu.SemaphoreType.DMA((nrow,)),
            pltpu.SemaphoreType.DMA((nrow,)),
        ],
        compiler_params=pltpu.CompilerParams(
            collective_id=0, has_side_effects=True, vmem_limit_bytes=48 * 1024 * 1024
        ),
        cost_estimate=pl.CostEstimate(
            flops=24 * width**3, bytes_accessed=6 * rows * slots * tile_size, transcendentals=0
        ),
    )(upper_tiles.swapaxes(0, 1).reshape(slots, rows, block // 2, lanes), block_columns)
    return new.reshape(slots, rows, tile_size).swapaxes(0, 1), occupancy[0, 0]


def solution(mesh):
    placed = (P(("row", "col"), None, None), P(("row", "col"), None))
    return jax.shard_map(
        functools.partial(body, mesh.shape["row"], mesh.shape["col"]),
        mesh=mesh,
        in_specs=placed,
        out_specs=(P(("row", "col"), None, None), P()),
        check_vma=False,
    )
```

```python
import functools
import math

import jax
import jax.numpy as jnp
from jax import lax
from jax.experimental import pallas as pl
from jax.experimental.pallas import tpu as pltpu
from jax.sharding import PartitionSpec as P

MESH = pl.DeviceIdType.MESH
F32 = jnp.float32
BF16 = jnp.bfloat16


def dot(a, b, ca, cb):
    return lax.dot_general(a, b, (((ca,), (cb,)), ((), ())), preferred_element_type=F32)


def kernel(
    dims,
    x_ref,
    cols_ref,
    out_ref,
    occupancy_ref,
    tab,
    stage,
    flat,
    own,
    e1,
    f1,
    e2,
    d1,
    c1,
    d2,
    prod,
    col_parts,
    row_parts,
    send_sem,
    recv_sem,
    col_send,
    col_recv,
    row_send,
    row_recv,
):
    rows, slots, block, nrow, ncol = dims
    half = slots - 1
    width = rows * block
    span = rows + half
    devices = nrow * ncol
    nblocks = devices * rows
    lanes = 2 * block
    strips = rows // 2
    my_row = lax.axis_index("row")
    my_col = lax.axis_index("col")
    me = my_row * ncol + my_col
    even_device = lax.rem(my_col, 2) == 0

    def at(shift):
        other = lax.rem(me + shift + devices, devices)
        return (lax.div(other, ncol), lax.rem(other, ncol))

    def col_peer(d):
        return lax.rem(my_col + d, ncol)

    def row_peer(d):
        return lax.rem(my_row + d, nrow)

    barrier = pltpu.get_barrier_semaphore()
    peers = [at(shift) for shift in (-2, -1, 1, 2)]
    peers += [(my_row, col_peer(d)) for d in range(1, ncol)]
    peers += [(row_peer(d), my_col) for d in range(1, nrow)]
    for peer in peers:
        pl.semaphore_signal(barrier, inc=1, device_id=peer, device_id_type=MESH)

    def fill(r, carry):
        row_id = me * rows + r
        tab[r, 0] = jnp.where(cols_ref[r, 0] >= 0, 0, -1).astype(jnp.int32)
        slot = jnp.int32(1)
        for offset in range(1, half + 1):
            want = row_id + offset
            want = jnp.where(want >= nblocks, want - nblocks, want)
            hit = cols_ref[r, jnp.minimum(slot, half)] == want
            tab[r, offset] = jnp.where(hit, slot, -1)
            slot = slot + hit.astype(jnp.int32)
        return carry

    lax.fori_loop(0, rows, fill, 0)

    sub = lax.broadcasted_iota(jnp.int32, (block // 2, lanes), 0)
    lane = lax.broadcasted_iota(jnp.int32, (block // 2, lanes), 1)
    left = lane < block
    on_diagonal = lane == 2 * sub + jnp.where(left, 0, block + 1)

    targets = {"f1": (f1, 2, 1, "low"), "d1": (d1, 0, -1, "up"), "e2": (e2, 2, 2, "low"),
               "d2": (d2, 0, -2, "up"), "e1": (e1, 1, 1, "full"), "c1": (c1, 1, -1, "full")}
    order = tuple(targets)

    def ranges(kind, q):
        lo = q * lanes if kind == "up" else 0
        return lo, {"full": width, "up": width - q * lanes, "low": (q + 1) * lanes}[kind]

    def strip_copy(name, q):
        target, part, shift, kind = targets[name]
        lo, size = ranges(kind, q)
        return pltpu.make_async_remote_copy(
            src_ref=own.at[pl.ds(q * lanes, lanes), pl.ds(part * width + lo, size)],
            dst_ref=target.at[pl.ds(q * lanes, lanes), pl.ds(lo, size)],
            send_sem=send_sem.at[order.index(name), q],
            recv_sem=recv_sem.at[order.index(name), q],
            device_id=at(shift),
            device_id_type=MESH,
        )

    def forward_copy(name, q):
        source, goal, shift = (f1, "e2", 1) if name == "f1" else (d1, "d2", -1)
        lo, size = ranges(targets[name][3], q)
        where = (pl.ds(q * lanes, lanes), pl.ds(lo, size))
        return pltpu.make_async_remote_copy(
            src_ref=source.at[where],
            dst_ref=targets[goal][0].at[where],
            send_sem=send_sem.at[len(order), q],
            recv_sem=recv_sem.at[order.index(goal), q],
            device_id=at(shift),
            device_id_type=MESH,
        )

    total = jnp.zeros((block // 2, lanes), F32)
    for q in range(strips):
        for r in (2 * q, 2 * q + 1):
            for m in range(span // 2):
                cs = slice(m * lanes, (m + 1) * lanes)
                pair = []
                for k in (2 * m, 2 * m + 1):
                    offset = k - r
                    if offset < 0 or offset > half:
                        pair.append(None)
                        continue
                    slot = tab[r, offset]
                    tile = x_ref[jnp.clip(slot, 0, half), r].astype(F32)
                    tile = jnp.where(slot >= 0, tile, 0.0)
                    if offset == 0:
                        total = total + jnp.where(on_diagonal, 2.0 * tile, 0.0) - tile * tile
                    else:
                        total = total - 2.0 * (tile * tile)
                    pair.append(tile)
                if pair[0] is None and pair[1] is None:
                    own[r * block : (r + 1) * block, cs] = jnp.zeros((block, lanes), BF16)
                    continue
                pair = [jnp.zeros((block // 2, lanes), F32) if t is None else t for t in pair]
                place = (r % 2) * (span // 2) + m
                stage[place, pl.ds(0, block // 2, stride=2), :] = jnp.where(left, pair[0], pltpu.roll(pair[1], block, 1))
                stage[place, pl.ds(1, block // 2, stride=2), :] = jnp.where(left, pltpu.roll(pair[0], block, 1), pair[1])
                own[r * block : (r + 1) * block, cs] = stage[place].astype(BF16)
        if q == 0:
            pl.semaphore_wait(barrier, len(peers))
        strip_copy("f1", q).start()
        strip_copy("d1", q).start()

        @pl.when(even_device)
        def _():
            strip_copy("e2", q).start()

        @pl.when(jnp.logical_not(even_device))
        def _():
            strip_copy("d2", q).start()

    for q in range(strips):
        strip_copy("e1", q).start()
        strip_copy("c1", q).start()

    part = total[0:8]
    for i in range(1, block // 16):
        part = part + total[8 * i : 8 * i + 8]

    def col_copy(d, mine):
        return pltpu.make_async_remote_copy(
            src_ref=col_parts.at[my_col],
            dst_ref=col_parts.at[my_col if mine else col_peer(ncol - d)],
            send_sem=col_send.at[d],
            recv_sem=col_recv.at[d],
            device_id=(my_row, col_peer(d)),
            device_id_type=MESH,
        )

    def row_copy(d, mine):
        return pltpu.make_async_remote_copy(
            src_ref=row_parts.at[my_row],
            dst_ref=row_parts.at[my_row if mine else row_peer(nrow - d)],
            send_sem=row_send.at[d],
            recv_sem=row_recv.at[d],
            device_id=(row_peer(d), my_col),
            device_id_type=MESH,
        )

    col_parts[my_col] = part
    for d in range(1, ncol):
        col_copy(d, True).start()

    def panel(i):
        return prod.at[:, i * width : (i + 1) * width]

    p0, p1, p2 = panel(0), panel(1), panel(2)
    d = own.at[:, :width]
    a = own.at[:, width : 2 * width]
    b = own.at[:, 2 * width :]

    corner = (
        lax.broadcasted_iota(jnp.int32, (lanes, lanes), 0) // block
        <= lax.broadcasted_iota(jnp.int32, (lanes, lanes), 1) // block
    )

    def symmetric_tile(upper):
        upper = upper.astype(F32)
        return jnp.where(corner, upper, upper.T).astype(BF16)

    def times_symmetric(x, u, p, q):
        lo, hi = q * lanes, (q + 1) * lanes
        rs = slice(lo, hi)
        tile = symmetric_tile(u[rs, lo:hi])
        p[:, rs] += dot(x[:, rs], tile, 1, 0)
        if hi < width:
            p[:, rs] += dot(x[:, hi:], u[rs, hi:], 1, 1)
            p[:, hi:] += dot(x[:, rs], u[rs, hi:], 1, 0)

    p0[...] = dot(a[...], a[...], 1, 1) + dot(b[...], b[...], 1, 1)
    full = d[...].astype(F32)
    block_upper = (
        lax.broadcasted_iota(jnp.int32, (width, width), 0) // block
        <= lax.broadcasted_iota(jnp.int32, (width, width), 1) // block
    )
    full = jnp.where(block_upper, full, full.T).astype(BF16)
    p0[...] += dot(full, full, 1, 0)
    p1[...] = dot(full, a[...], 1, 0)
    p2[...] = dot(full, b[...], 1, 0)

    def far(q):
        low = slice(0, (q + 1) * lanes)
        strip_copy("e2", q).wait_recv()
        p0[low, low] += dot(e2[q * lanes : (q + 1) * lanes, low], e2[q * lanes : (q + 1) * lanes, low], 0, 0)
        strip_copy("d2", q).wait_recv()
        times_symmetric(b, d2, p2, q)

    for q in range(strips):
        strip_copy("f1", q).wait_recv()

        @pl.when(even_device)
        def _():
            forward_copy("f1", q).start()

        strip_copy("d1", q).wait_recv()

        @pl.when(jnp.logical_not(even_device))
        def _():
            forward_copy("d1", q).start()

        times_symmetric(a, d1, p1, q)
        if q:
            far(q - 1)
    far(strips - 1)

    for i in range(1, ncol):
        col_copy(i, False).wait_recv()
    part = col_parts[0]
    for i in range(1, ncol):
        part = part + col_parts[i]
    row_parts[my_row] = part
    for i in range(1, nrow):
        row_copy(i, True).start()

    for q in range(strips):
        rs = slice(q * lanes, (q + 1) * lanes)
        low = slice(0, (q + 1) * lanes)
        strip_copy("c1", q).wait_recv()
        p1[:, rs] += dot(b[...], c1[rs, :], 1, 1)
        p2[...] += dot(a[:, rs], c1[rs, :], 1, 0)
        strip_copy("e1", q).wait_recv()
        p0[...] += dot(e1[rs, :], e1[rs, :], 0, 0)
        p1[:, low] += dot(e1[rs, :], f1[rs, low], 0, 0)

    for r in range(rows):
        for m in range(r // 2, (r + half) // 2 + 1):
            cs = slice(m * lanes, (m + 1) * lanes)
            place = (r % 2) * (span // 2) + m
            stage[place] = prod[r * block : (r + 1) * block, cs]
            even = stage[place, pl.ds(0, block // 2, stride=2), :]
            odd = stage[place, pl.ds(1, block // 2, stride=2), :]
            flat[r, 2 * m] = jnp.where(left, even, pltpu.roll(odd, block, 1))
            flat[r, 2 * m + 1] = jnp.where(left, pltpu.roll(even, block, 1), odd)

    def pick(r, carry):
        row_id = me * rows + r
        for s in range(slots):
            column = cols_ref[r, s]
            offset = column - row_id
            offset = jnp.where(offset < 0, offset + nblocks, offset)
            offset = jnp.where(column >= 0, jnp.minimum(offset, half), 0)
            fresh = 2.0 * x_ref[s, r].astype(F32) - flat[r, r + offset]
            out_ref[s, r] = jnp.where(column >= 0, fresh, 0.0)
        return carry

    lax.fori_loop(0, rows, pick, 0)

    for i in range(1, nrow):
        row_copy(i, False).wait_recv()
    part = row_parts[0]
    for i in range(1, nrow):
        part = part + row_parts[i]
    occupancy_ref[0, 0] = jnp.sum(part) * (1.0 / (nblocks * block))

    for q in range(strips):
        for name in ("f1", "d1", "e1", "c1"):
            strip_copy(name, q).wait_send()

        @pl.when(even_device)
        def _():
            strip_copy("e2", q).wait_send()
            forward_copy("f1", q).wait_send()

        @pl.when(jnp.logical_not(even_device))
        def _():
            strip_copy("d2", q).wait_send()
            forward_copy("d1", q).wait_send()

    for i in range(1, ncol):
        col_copy(i, True).wait_send()
    for i in range(1, nrow):
        row_copy(i, True).wait_send()


def body(nrow, ncol, upper_tiles, block_columns):
    rows, slots, tile_size = upper_tiles.shape
    block = math.isqrt(tile_size)
    half = slots - 1
    assert half == 2 * rows and rows % 2 == 0 and 2 * block == 128 and ncol % 2 == 0
    lanes = 2 * block
    width = rows * block
    span = rows + half
    strips = rows // 2

    square = pltpu.VMEM((width, width), BF16)
    new, occupancy = pl.pallas_call(
        functools.partial(kernel, (rows, slots, block, nrow, ncol)),
        out_shape=(
            jax.ShapeDtypeStruct((slots, rows, block // 2, lanes), F32),
            jax.ShapeDtypeStruct((1, 1), F32),
        ),
        in_specs=[pl.BlockSpec(memory_space=pltpu.VMEM), pl.BlockSpec(memory_space=pltpu.SMEM)],
        out_specs=(pl.BlockSpec(memory_space=pltpu.VMEM), pl.BlockSpec(memory_space=pltpu.SMEM)),
        scratch_shapes=[
            pltpu.SMEM((rows, slots), jnp.int32),
            pltpu.VMEM((span, block, lanes), F32),
            pltpu.VMEM((rows, span, block // 2, lanes), F32),
            pltpu.VMEM((width, 3 * width), BF16),
            square,
            square,
            square,
            square,
            square,
            square,
            pltpu.VMEM((width, 3 * width), F32),
            pltpu.VMEM((ncol, 8, lanes), F32),
            pltpu.VMEM((nrow, 8, lanes), F32),
            pltpu.SemaphoreType.DMA((7, strips)),
            pltpu.SemaphoreType.DMA((6, strips)),
            pltpu.SemaphoreType.DMA((ncol,)),
            pltpu.SemaphoreType.DMA((ncol,)),
            pltpu.SemaphoreType.DMA((nrow,)),
            pltpu.SemaphoreType.DMA((nrow,)),
        ],
        compiler_params=pltpu.CompilerParams(
            collective_id=0, has_side_effects=True, vmem_limit_bytes=48 * 1024 * 1024
        ),
        cost_estimate=pl.CostEstimate(
            flops=24 * width**3, bytes_accessed=6 * rows * slots * tile_size, transcendentals=0
        ),
    )(upper_tiles.swapaxes(0, 1).reshape(slots, rows, block // 2, lanes), block_columns)
    return new.reshape(slots, rows, tile_size).swapaxes(0, 1), occupancy[0, 0]


def solution(mesh):
    placed = (P(("row", "col"), None, None), P(("row", "col"), None))
    return jax.shard_map(
        functools.partial(body, mesh.shape["row"], mesh.shape["col"]),
        mesh=mesh,
        in_specs=placed,
        out_specs=(P(("row", "col"), None, None), P()),
        check_vma=False,
    )
```

```python
import functools
import math

import jax
import jax.numpy as jnp
from jax import lax
from jax.experimental import pallas as pl
from jax.experimental.pallas import tpu as pltpu
from jax.sharding import PartitionSpec as P

MESH = pl.DeviceIdType.MESH
F32 = jnp.float32
BF16 = jnp.bfloat16


def dot(a, b, ca, cb):
    return lax.dot_general(a, b, (((ca,), (cb,)), ((), ())), preferred_element_type=F32)


def kernel(
    dims,
    x_ref,
    cols_ref,
    out_ref,
    occupancy_ref,
    stage,
    flat,
    own,
    e1,
    f1,
    e2,
    d1,
    c1,
    d2,
    prod,
    col_parts,
    row_parts,
    send_sem,
    recv_sem,
    col_send,
    col_recv,
    row_send,
    row_recv,
):
    rows, slots, block, nrow, ncol = dims
    half = slots - 1
    width = rows * block
    span = rows + half
    devices = nrow * ncol
    nblocks = devices * rows
    lanes = 2 * block
    strips = rows // 2
    my_row = lax.axis_index("row")
    my_col = lax.axis_index("col")
    me = my_row * ncol + my_col
    even_device = lax.rem(my_col, 2) == 0

    def at(shift):
        other = lax.rem(me + shift + devices, devices)
        return (lax.div(other, ncol), lax.rem(other, ncol))

    def col_peer(d):
        return lax.rem(my_col + d, ncol)

    def row_peer(d):
        return lax.rem(my_row + d, nrow)

    barrier = pltpu.get_barrier_semaphore()
    peers = [at(shift) for shift in (-2, -1, 1, 2)]
    peers += [(my_row, col_peer(d)) for d in range(1, ncol)]
    peers += [(row_peer(d), my_col) for d in range(1, nrow)]
    for peer in peers:
        pl.semaphore_signal(barrier, inc=1, device_id=peer, device_id_type=MESH)

    def slots_of(r):
        row_id = me * rows + r
        found = [jnp.where(cols_ref[r, 0] >= 0, 0, -1).astype(jnp.int32)]
        slot = jnp.int32(1)
        for offset in range(1, half + 1):
            want = row_id + offset
            want = jnp.where(want >= nblocks, want - nblocks, want)
            hit = cols_ref[r, jnp.minimum(slot, half)] == want
            found.append(jnp.where(hit, slot, -1))
            slot = slot + hit.astype(jnp.int32)
        return found

    sub = lax.broadcasted_iota(jnp.int32, (block // 2, lanes), 0)
    lane = lax.broadcasted_iota(jnp.int32, (block // 2, lanes), 1)
    left = lane < block
    on_diagonal = lane == 2 * sub + jnp.where(left, 0, block + 1)

    targets = {"f1": (f1, 2, 1, "low"), "d1": (d1, 0, -1, "up"), "e2": (e2, 2, 2, "low"),
               "d2": (d2, 0, -2, "up"), "e1": (e1, 1, 1, "full"), "c1": (c1, 1, -1, "full")}
    order = tuple(targets)

    def ranges(kind, q):
        lo = q * lanes if kind == "up" else 0
        return lo, {"full": width, "up": width - q * lanes, "low": (q + 1) * lanes}[kind]

    def strip_copy(name, q):
        target, part, shift, kind = targets[name]
        lo, size = ranges(kind, q)
        return pltpu.make_async_remote_copy(
            src_ref=own.at[pl.ds(q * lanes, lanes), pl.ds(part * width + lo, size)],
            dst_ref=target.at[pl.ds(q * lanes, lanes), pl.ds(lo, size)],
            send_sem=send_sem.at[order.index(name), q],
            recv_sem=recv_sem.at[order.index(name), q],
            device_id=at(shift),
            device_id_type=MESH,
        )

    def forward_copy(name, q):
        source, goal, shift = (f1, "e2", 1) if name == "f1" else (d1, "d2", -1)
        lo, size = ranges(targets[name][3], q)
        where = (pl.ds(q * lanes, lanes), pl.ds(lo, size))
        return pltpu.make_async_remote_copy(
            src_ref=source.at[where],
            dst_ref=targets[goal][0].at[where],
            send_sem=send_sem.at[len(order), q],
            recv_sem=recv_sem.at[order.index(goal), q],
            device_id=at(shift),
            device_id_type=MESH,
        )

    total = jnp.zeros((block // 2, lanes), F32)
    for q in range(strips):
        for r in (2 * q, 2 * q + 1):
            found = slots_of(r)
            for m in range(span // 2):
                cs = slice(m * lanes, (m + 1) * lanes)
                pair = []
                for k in (2 * m, 2 * m + 1):
                    offset = k - r
                    if offset < 0 or offset > half:
                        pair.append(None)
                        continue
                    slot = found[offset]
                    tile = x_ref[jnp.clip(slot, 0, half), r].astype(F32)
                    tile = jnp.where(slot >= 0, tile, 0.0)
                    if offset == 0:
                        total = total + jnp.where(on_diagonal, 2.0 * tile, 0.0) - tile * tile
                    else:
                        total = total - 2.0 * (tile * tile)
                    pair.append(tile)
                if pair[0] is None and pair[1] is None:
                    own[r * block : (r + 1) * block, cs] = jnp.zeros((block, lanes), BF16)
                    continue
                pair = [jnp.zeros((block // 2, lanes), F32) if t is None else t for t in pair]
                place = (r % 2) * (span // 2) + m
                stage[place, pl.ds(0, block // 2, stride=2), :] = jnp.where(left, pair[0], pltpu.roll(pair[1], block, 1))
                stage[place, pl.ds(1, block // 2, stride=2), :] = jnp.where(left, pltpu.roll(pair[0], block, 1), pair[1])
                own[r * block : (r + 1) * block, cs] = stage[place].astype(BF16)
        if q == 0:
            pl.semaphore_wait(barrier, len(peers))
        strip_copy("f1", q).start()
        strip_copy("d1", q).start()

        @pl.when(even_device)
        def _():
            strip_copy("e2", q).start()

        @pl.when(jnp.logical_not(even_device))
        def _():
            strip_copy("d2", q).start()

    for q in range(strips):
        strip_copy("e1", q).start()
        strip_copy("c1", q).start()

    part = total[0:8]
    for i in range(1, block // 16):
        part = part + total[8 * i : 8 * i + 8]

    def col_copy(d, mine):
        return pltpu.make_async_remote_copy(
            src_ref=col_parts.at[my_col],
            dst_ref=col_parts.at[my_col if mine else col_peer(ncol - d)],
            send_sem=col_send.at[d],
            recv_sem=col_recv.at[d],
            device_id=(my_row, col_peer(d)),
            device_id_type=MESH,
        )

    def row_copy(d, mine):
        return pltpu.make_async_remote_copy(
            src_ref=row_parts.at[my_row],
            dst_ref=row_parts.at[my_row if mine else row_peer(nrow - d)],
            send_sem=row_send.at[d],
            recv_sem=row_recv.at[d],
            device_id=(row_peer(d), my_col),
            device_id_type=MESH,
        )

    col_parts[my_col] = part
    for d in range(1, ncol):
        col_copy(d, True).start()

    def panel(i):
        return prod.at[:, i * width : (i + 1) * width]

    p0, p1, p2 = panel(0), panel(1), panel(2)
    d = own.at[:, :width]
    a = own.at[:, width : 2 * width]
    b = own.at[:, 2 * width :]

    corner = (
        lax.broadcasted_iota(jnp.int32, (lanes, lanes), 0) // block
        <= lax.broadcasted_iota(jnp.int32, (lanes, lanes), 1) // block
    )

    def symmetric_tile(upper):
        upper = upper.astype(F32)
        return jnp.where(corner, upper, upper.T).astype(BF16)

    def times_symmetric(x, u, p, q):
        lo, hi = q * lanes, (q + 1) * lanes
        rs = slice(lo, hi)
        tile = symmetric_tile(u[rs, lo:hi])
        p[:, rs] += dot(x[:, rs], tile, 1, 0)
        if hi < width:
            p[:, rs] += dot(x[:, hi:], u[rs, hi:], 1, 1)
            p[:, hi:] += dot(x[:, rs], u[rs, hi:], 1, 0)

    p0[...] = dot(a[...], a[...], 1, 1) + dot(b[...], b[...], 1, 1)
    full = d[...].astype(F32)
    block_upper = (
        lax.broadcasted_iota(jnp.int32, (width, width), 0) // block
        <= lax.broadcasted_iota(jnp.int32, (width, width), 1) // block
    )
    full = jnp.where(block_upper, full, full.T).astype(BF16)
    p0[...] += dot(full, full, 1, 0)
    p1[...] = dot(full, a[...], 1, 0)
    p2[...] = dot(full, b[...], 1, 0)

    def far(q):
        low = slice(0, (q + 1) * lanes)
        strip_copy("e2", q).wait_recv()
        p0[low, low] += dot(e2[q * lanes : (q + 1) * lanes, low], e2[q * lanes : (q + 1) * lanes, low], 0, 0)
        strip_copy("d2", q).wait_recv()
        times_symmetric(b, d2, p2, q)

    for q in range(strips):
        strip_copy("f1", q).wait_recv()

        @pl.when(even_device)
        def _():
            forward_copy("f1", q).start()

        strip_copy("d1", q).wait_recv()

        @pl.when(jnp.logical_not(even_device))
        def _():
            forward_copy("d1", q).start()

        times_symmetric(a, d1, p1, q)
        if q:
            far(q - 1)
    far(strips - 1)

    for i in range(1, ncol):
        col_copy(i, False).wait_recv()
    part = col_parts[0]
    for i in range(1, ncol):
        part = part + col_parts[i]
    row_parts[my_row] = part
    for i in range(1, nrow):
        row_copy(i, True).start()

    def above(q):
        rs = slice(q * lanes, (q + 1) * lanes)
        strip_copy("c1", q).wait_recv()
        p1[:, rs] += dot(b[...], c1[rs, :], 1, 1)
        p2[...] += dot(a[:, rs], c1[rs, :], 1, 0)

    def below(q):
        rs = slice(q * lanes, (q + 1) * lanes)
        low = slice(0, (q + 1) * lanes)
        strip_copy("e1", q).wait_recv()
        p0[...] += dot(e1[rs, :], e1[rs, :], 0, 0)
        p1[:, low] += dot(e1[rs, :], f1[rs, low], 0, 0)

    def pack(first, last):
        for r in range(rows):
            for m in range(max(r // 2, first * strips), min((r + half) // 2, (last + 1) * strips - 1) + 1):
                cs = slice(m * lanes, (m + 1) * lanes)
                place = (r % 2) * (span // 2) + m
                stage[place] = prod[r * block : (r + 1) * block, cs]
                even = stage[place, pl.ds(0, block // 2, stride=2), :]
                odd = stage[place, pl.ds(1, block // 2, stride=2), :]
                flat[r, 2 * m] = jnp.where(left, even, pltpu.roll(odd, block, 1))
                flat[r, 2 * m + 1] = jnp.where(left, pltpu.roll(even, block, 1), odd)

    @pl.when(even_device)
    def _():
        for q in range(strips):
            above(q)
        pack(2, 2)
        for q in range(strips):
            below(q)
        pack(0, 1)

    @pl.when(jnp.logical_not(even_device))
    def _():
        for q in range(strips):
            below(q)
        pack(0, 0)
        for q in range(strips):
            above(q)
        pack(1, 2)

    def pick(r, carry):
        row_id = me * rows + r
        for s in range(slots):
            column = cols_ref[r, s]
            offset = column - row_id
            offset = jnp.where(offset < 0, offset + nblocks, offset)
            offset = jnp.where(column >= 0, jnp.minimum(offset, half), 0)
            fresh = 2.0 * x_ref[s, r].astype(F32) - flat[r, r + offset]
            out_ref[s, r] = jnp.where(column >= 0, fresh, 0.0)
        return carry

    lax.fori_loop(0, rows, pick, 0)

    for i in range(1, nrow):
        row_copy(i, False).wait_recv()
    part = row_parts[0]
    for i in range(1, nrow):
        part = part + row_parts[i]
    occupancy_ref[0, 0] = jnp.sum(part) * (1.0 / (nblocks * block))

    for q in range(strips):
        for name in ("f1", "d1", "e1", "c1"):
            strip_copy(name, q).wait_send()

        @pl.when(even_device)
        def _():
            strip_copy("e2", q).wait_send()
            forward_copy("f1", q).wait_send()

        @pl.when(jnp.logical_not(even_device))
        def _():
            strip_copy("d2", q).wait_send()
            forward_copy("d1", q).wait_send()

    for i in range(1, ncol):
        col_copy(i, True).wait_send()
    for i in range(1, nrow):
        row_copy(i, True).wait_send()


def body(nrow, ncol, upper_tiles, block_columns):
    rows, slots, tile_size = upper_tiles.shape
    block = math.isqrt(tile_size)
    half = slots - 1
    assert half == 2 * rows and rows % 2 == 0 and 2 * block == 128 and ncol % 2 == 0
    lanes = 2 * block
    width = rows * block
    span = rows + half
    strips = rows // 2

    square = pltpu.VMEM((width, width), BF16)
    new, occupancy = pl.pallas_call(
        functools.partial(kernel, (rows, slots, block, nrow, ncol)),
        out_shape=(
            jax.ShapeDtypeStruct((slots, rows, block // 2, lanes), F32),
            jax.ShapeDtypeStruct((1, 1), F32),
        ),
        in_specs=[pl.BlockSpec(memory_space=pltpu.VMEM), pl.BlockSpec(memory_space=pltpu.SMEM)],
        out_specs=(pl.BlockSpec(memory_space=pltpu.VMEM), pl.BlockSpec(memory_space=pltpu.SMEM)),
        scratch_shapes=[
            pltpu.VMEM((span, block, lanes), F32),
            pltpu.VMEM((rows, span, block // 2, lanes), F32),
            pltpu.VMEM((width, 3 * width), BF16),
            square,
            square,
            square,
            square,
            square,
            square,
            pltpu.VMEM((width, 3 * width), F32),
            pltpu.VMEM((ncol, 8, lanes), F32),
            pltpu.VMEM((nrow, 8, lanes), F32),
            pltpu.SemaphoreType.DMA((7, strips)),
            pltpu.SemaphoreType.DMA((6, strips)),
            pltpu.SemaphoreType.DMA((ncol,)),
            pltpu.SemaphoreType.DMA((ncol,)),
            pltpu.SemaphoreType.DMA((nrow,)),
            pltpu.SemaphoreType.DMA((nrow,)),
        ],
        compiler_params=pltpu.CompilerParams(
            collective_id=0, has_side_effects=True, vmem_limit_bytes=48 * 1024 * 1024
        ),
        cost_estimate=pl.CostEstimate(
            flops=24 * width**3, bytes_accessed=6 * rows * slots * tile_size, transcendentals=0
        ),
    )(upper_tiles.swapaxes(0, 1).reshape(slots, rows, block // 2, lanes), block_columns)
    return new.reshape(slots, rows, tile_size).swapaxes(0, 1), occupancy[0, 0]


def solution(mesh):
    placed = (P(("row", "col"), None, None), P(("row", "col"), None))
    return jax.shard_map(
        functools.partial(body, mesh.shape["row"], mesh.shape["col"]),
        mesh=mesh,
        in_specs=placed,
        out_specs=(P(("row", "col"), None, None), P()),
        check_vma=False,
    )
```

```python
import functools
import math

import jax
import jax.numpy as jnp
from jax import lax
from jax.experimental import pallas as pl
from jax.experimental.pallas import tpu as pltpu
from jax.sharding import PartitionSpec as P

MESH = pl.DeviceIdType.MESH
F32 = jnp.float32
BF16 = jnp.bfloat16


def dot(a, b, ca, cb):
    return lax.dot_general(a, b, (((ca,), (cb,)), ((), ())), preferred_element_type=F32)


def kernel(
    dims,
    x_ref,
    cols_ref,
    out_ref,
    occupancy_ref,
    stage,
    flat,
    own,
    e1,
    f1,
    e2,
    d1,
    c1,
    d2,
    prod,
    col_parts,
    row_parts,
    send_sem,
    recv_sem,
    col_send,
    col_recv,
    row_send,
    row_recv,
):
    rows, slots, block, nrow, ncol = dims
    half = slots - 1
    width = rows * block
    span = rows + half
    devices = nrow * ncol
    nblocks = devices * rows
    lanes = 2 * block
    strips = rows // 2
    my_row = lax.axis_index("row")
    my_col = lax.axis_index("col")
    me = my_row * ncol + my_col
    even_device = lax.rem(my_col, 2) == 0

    def at(shift):
        other = lax.rem(me + shift + devices, devices)
        return (lax.div(other, ncol), lax.rem(other, ncol))

    def col_peer(d):
        return lax.rem(my_col + d, ncol)

    def row_peer(d):
        return lax.rem(my_row + d, nrow)

    barrier = pltpu.get_barrier_semaphore()
    peers = [at(shift) for shift in (-2, -1, 1, 2)]
    peers += [(my_row, col_peer(d)) for d in range(1, ncol)]
    peers += [(row_peer(d), my_col) for d in range(1, nrow)]
    for peer in peers:
        pl.semaphore_signal(barrier, inc=1, device_id=peer, device_id_type=MESH)

    def slots_of(r):
        row_id = me * rows + r
        found = [jnp.where(cols_ref[r, 0] >= 0, 0, -1).astype(jnp.int32)]
        slot = jnp.int32(1)
        for offset in range(1, half + 1):
            want = row_id + offset
            want = jnp.where(want >= nblocks, want - nblocks, want)
            hit = cols_ref[r, jnp.minimum(slot, half)] == want
            found.append(jnp.where(hit, slot, -1))
            slot = slot + hit.astype(jnp.int32)
        return found

    sub = lax.broadcasted_iota(jnp.int32, (block // 2, lanes), 0)
    lane = lax.broadcasted_iota(jnp.int32, (block // 2, lanes), 1)
    left = lane < block
    on_diagonal = lane == 2 * sub + jnp.where(left, 0, block + 1)

    targets = {"f1": (f1, 2, 1, "low"), "d1": (d1, 0, -1, "up"), "e2": (e2, 2, 2, "low"),
               "d2": (d2, 0, -2, "up"), "e1": (e1, 1, 1, "full"), "c1": (c1, 1, -1, "full")}
    order = tuple(targets)

    def ranges(kind, q):
        lo = q * lanes if kind == "up" else 0
        return lo, {"full": width, "up": width - q * lanes, "low": (q + 1) * lanes}[kind]

    def strip_copy(name, q):
        target, part, shift, kind = targets[name]
        lo, size = ranges(kind, q)
        return pltpu.make_async_remote_copy(
            src_ref=own.at[pl.ds(q * lanes, lanes), pl.ds(part * width + lo, size)],
            dst_ref=target.at[pl.ds(q * lanes, lanes), pl.ds(lo, size)],
            send_sem=send_sem.at[order.index(name), q],
            recv_sem=recv_sem.at[order.index(name), q],
            device_id=at(shift),
            device_id_type=MESH,
        )

    def forward_copy(name, q):
        source, goal, shift = (f1, "e2", 1) if name == "f1" else (d1, "d2", -1)
        lo, size = ranges(targets[name][3], q)
        where = (pl.ds(q * lanes, lanes), pl.ds(lo, size))
        return pltpu.make_async_remote_copy(
            src_ref=source.at[where],
            dst_ref=targets[goal][0].at[where],
            send_sem=send_sem.at[len(order), q],
            recv_sem=recv_sem.at[order.index(goal), q],
            device_id=at(shift),
            device_id_type=MESH,
        )

    total = jnp.zeros((block // 2, lanes), F32)
    for q in range(strips):
        for r in (2 * q, 2 * q + 1):
            found = slots_of(r)
            for m in range(span // 2):
                cs = slice(m * lanes, (m + 1) * lanes)
                pair = []
                for k in (2 * m, 2 * m + 1):
                    offset = k - r
                    if offset < 0 or offset > half:
                        pair.append(None)
                        continue
                    slot = found[offset]
                    tile = x_ref[jnp.clip(slot, 0, half), r].astype(F32)
                    tile = jnp.where(slot >= 0, tile, 0.0)
                    if offset == 0:
                        total = total + jnp.where(on_diagonal, 2.0 * tile, 0.0) - tile * tile
                    else:
                        total = total - 2.0 * (tile * tile)
                    pair.append(tile)
                if pair[0] is None and pair[1] is None:
                    own[r * block : (r + 1) * block, cs] = jnp.zeros((block, lanes), BF16)
                    continue
                pair = [jnp.zeros((block // 2, lanes), F32) if t is None else t for t in pair]
                place = (r % 2) * (span // 2) + m
                stage[place, pl.ds(0, block // 2, stride=2), :] = jnp.where(left, pair[0], pltpu.roll(pair[1], block, 1))
                stage[place, pl.ds(1, block // 2, stride=2), :] = jnp.where(left, pltpu.roll(pair[0], block, 1), pair[1])
                own[r * block : (r + 1) * block, cs] = stage[place].astype(BF16)
        if q == 0:
            pl.semaphore_wait(barrier, len(peers))
        strip_copy("f1", q).start()
        strip_copy("d1", q).start()

        @pl.when(even_device)
        def _():
            strip_copy("e2", q).start()

        @pl.when(jnp.logical_not(even_device))
        def _():
            strip_copy("d2", q).start()

    part = total[0:8]
    for i in range(1, block // 16):
        part = part + total[8 * i : 8 * i + 8]

    def col_copy(d, mine):
        return pltpu.make_async_remote_copy(
            src_ref=col_parts.at[my_col],
            dst_ref=col_parts.at[my_col if mine else col_peer(ncol - d)],
            send_sem=col_send.at[d],
            recv_sem=col_recv.at[d],
            device_id=(my_row, col_peer(d)),
            device_id_type=MESH,
        )

    def row_copy(d, mine):
        return pltpu.make_async_remote_copy(
            src_ref=row_parts.at[my_row],
            dst_ref=row_parts.at[my_row if mine else row_peer(nrow - d)],
            send_sem=row_send.at[d],
            recv_sem=row_recv.at[d],
            device_id=(row_peer(d), my_col),
            device_id_type=MESH,
        )

    col_parts[my_col] = part
    for d in range(1, ncol):
        col_copy(d, True).start()

    def panel(i):
        return prod.at[:, i * width : (i + 1) * width]

    p0, p1, p2 = panel(0), panel(1), panel(2)
    d = own.at[:, :width]
    a = own.at[:, width : 2 * width]
    b = own.at[:, 2 * width :]

    corner = (
        lax.broadcasted_iota(jnp.int32, (lanes, lanes), 0) // block
        <= lax.broadcasted_iota(jnp.int32, (lanes, lanes), 1) // block
    )

    def symmetric_tile(upper):
        upper = upper.astype(F32)
        return jnp.where(corner, upper, upper.T).astype(BF16)

    def times_symmetric(x, u, p, q):
        lo, hi = q * lanes, (q + 1) * lanes
        rs = slice(lo, hi)
        tile = symmetric_tile(u[rs, lo:hi])
        p[:, rs] += dot(x[:, rs], tile, 1, 0)
        if hi < width:
            p[:, rs] += dot(x[:, hi:], u[rs, hi:], 1, 1)
            p[:, hi:] += dot(x[:, rs], u[rs, hi:], 1, 0)

    p0[...] = dot(a[...], a[...], 1, 1) + dot(b[...], b[...], 1, 1)
    full = d[...].astype(F32)
    block_upper = (
        lax.broadcasted_iota(jnp.int32, (width, width), 0) // block
        <= lax.broadcasted_iota(jnp.int32, (width, width), 1) // block
    )
    full = jnp.where(block_upper, full, full.T).astype(BF16)
    p0[...] += dot(full, full, 1, 0)
    p1[...] = dot(full, a[...], 1, 0)
    p2[...] = dot(full, b[...], 1, 0)

    for i in range(1, ncol):
        col_copy(i, False).wait_recv()
    part = col_parts[0]
    for i in range(1, ncol):
        part = part + col_parts[i]
    row_parts[my_row] = part
    for i in range(1, nrow):
        row_copy(i, True).start()

    for q in range(strips):
        strip_copy("e1", q).start()
        strip_copy("c1", q).start()

    def far(q):
        low = slice(0, (q + 1) * lanes)
        strip_copy("e2", q).wait_recv()
        p0[low, low] += dot(e2[q * lanes : (q + 1) * lanes, low], e2[q * lanes : (q + 1) * lanes, low], 0, 0)
        strip_copy("d2", q).wait_recv()
        times_symmetric(b, d2, p2, q)

    for q in range(strips):
        strip_copy("f1", q).wait_recv()

        @pl.when(even_device)
        def _():
            forward_copy("f1", q).start()

        strip_copy("d1", q).wait_recv()

        @pl.when(jnp.logical_not(even_device))
        def _():
            forward_copy("d1", q).start()

        times_symmetric(a, d1, p1, q)
        if q:
            far(q - 1)
    far(strips - 1)

    def above(q):
        rs = slice(q * lanes, (q + 1) * lanes)
        strip_copy("c1", q).wait_recv()
        p1[:, rs] += dot(b[...], c1[rs, :], 1, 1)
        p2[...] += dot(a[:, rs], c1[rs, :], 1, 0)

    def below(q):
        rs = slice(q * lanes, (q + 1) * lanes)
        low = slice(0, (q + 1) * lanes)
        strip_copy("e1", q).wait_recv()
        p0[...] += dot(e1[rs, :], e1[rs, :], 0, 0)
        p1[:, low] += dot(e1[rs, :], f1[rs, low], 0, 0)

    def pack(first, last):
        for r in range(rows):
            for m in range(max(r // 2, first * strips), min((r + half) // 2, (last + 1) * strips - 1) + 1):
                cs = slice(m * lanes, (m + 1) * lanes)
                place = (r % 2) * (span // 2) + m
                stage[place] = prod[r * block : (r + 1) * block, cs]
                even = stage[place, pl.ds(0, block // 2, stride=2), :]
                odd = stage[place, pl.ds(1, block // 2, stride=2), :]
                flat[r, 2 * m] = jnp.where(left, even, pltpu.roll(odd, block, 1))
                flat[r, 2 * m + 1] = jnp.where(left, pltpu.roll(even, block, 1), odd)

    @pl.when(even_device)
    def _():
        for q in range(strips):
            above(q)
        pack(2, 2)
        for q in range(strips):
            below(q)
        pack(0, 1)

    @pl.when(jnp.logical_not(even_device))
    def _():
        for q in range(strips):
            below(q)
        pack(0, 0)
        for q in range(strips):
            above(q)
        pack(1, 2)

    def pick(r, carry):
        row_id = me * rows + r
        for s in range(slots):
            column = cols_ref[r, s]
            offset = column - row_id
            offset = jnp.where(offset < 0, offset + nblocks, offset)
            offset = jnp.where(column >= 0, jnp.minimum(offset, half), 0)
            fresh = 2.0 * x_ref[s, r].astype(F32) - flat[r, r + offset]
            out_ref[s, r] = jnp.where(column >= 0, fresh, 0.0)
        return carry

    lax.fori_loop(0, rows, pick, 0)

    for i in range(1, nrow):
        row_copy(i, False).wait_recv()
    part = row_parts[0]
    for i in range(1, nrow):
        part = part + row_parts[i]
    occupancy_ref[0, 0] = jnp.sum(part) * (1.0 / (nblocks * block))

    for q in range(strips):
        for name in ("f1", "d1", "e1", "c1"):
            strip_copy(name, q).wait_send()

        @pl.when(even_device)
        def _():
            strip_copy("e2", q).wait_send()
            forward_copy("f1", q).wait_send()

        @pl.when(jnp.logical_not(even_device))
        def _():
            strip_copy("d2", q).wait_send()
            forward_copy("d1", q).wait_send()

    for i in range(1, ncol):
        col_copy(i, True).wait_send()
    for i in range(1, nrow):
        row_copy(i, True).wait_send()


def body(nrow, ncol, upper_tiles, block_columns):
    rows, slots, tile_size = upper_tiles.shape
    block = math.isqrt(tile_size)
    half = slots - 1
    assert half == 2 * rows and rows % 2 == 0 and 2 * block == 128 and ncol % 2 == 0
    lanes = 2 * block
    width = rows * block
    span = rows + half
    strips = rows // 2

    square = pltpu.VMEM((width, width), BF16)
    new, occupancy = pl.pallas_call(
        functools.partial(kernel, (rows, slots, block, nrow, ncol)),
        out_shape=(
            jax.ShapeDtypeStruct((slots, rows, block // 2, lanes), F32),
            jax.ShapeDtypeStruct((1, 1), F32),
        ),
        in_specs=[pl.BlockSpec(memory_space=pltpu.VMEM), pl.BlockSpec(memory_space=pltpu.SMEM)],
        out_specs=(pl.BlockSpec(memory_space=pltpu.VMEM), pl.BlockSpec(memory_space=pltpu.SMEM)),
        scratch_shapes=[
            pltpu.VMEM((span, block, lanes), F32),
            pltpu.VMEM((rows, span, block // 2, lanes), F32),
            pltpu.VMEM((width, 3 * width), BF16),
            square,
            square,
            square,
            square,
            square,
            square,
            pltpu.VMEM((width, 3 * width), F32),
            pltpu.VMEM((ncol, 8, lanes), F32),
            pltpu.VMEM((nrow, 8, lanes), F32),
            pltpu.SemaphoreType.DMA((7, strips)),
            pltpu.SemaphoreType.DMA((6, strips)),
            pltpu.SemaphoreType.DMA((ncol,)),
            pltpu.SemaphoreType.DMA((ncol,)),
            pltpu.SemaphoreType.DMA((nrow,)),
            pltpu.SemaphoreType.DMA((nrow,)),
        ],
        compiler_params=pltpu.CompilerParams(
            collective_id=0, has_side_effects=True, vmem_limit_bytes=48 * 1024 * 1024
        ),
        cost_estimate=pl.CostEstimate(
            flops=24 * width**3, bytes_accessed=6 * rows * slots * tile_size, transcendentals=0
        ),
    )(upper_tiles.swapaxes(0, 1).reshape(slots, rows, block // 2, lanes), block_columns)
    return new.reshape(slots, rows, tile_size).swapaxes(0, 1), occupancy[0, 0]


def solution(mesh):
    placed = (P(("row", "col"), None, None), P(("row", "col"), None))
    return jax.shard_map(
        functools.partial(body, mesh.shape["row"], mesh.shape["col"]),
        mesh=mesh,
        in_specs=placed,
        out_specs=(P(("row", "col"), None, None), P()),
        check_vma=False,
    )
```
